32 devices in a mesh: energy: 8 (over y, x, core), mom: 4 (over z).
Axes of the slice: x: 2, y: 2, z: 4, core: 2. Of those that a mesh axis runs over, the one named last changes fastest.
Arguments:
- green_ret: bfloat16 [8, 4, 12, 3, 2, 128, 128], P('energy', 'mom'), may hold values from -0.5 to 0.5
- sigma_in: bfloat16 [8, 4, 12, 2, 128, 128], P('energy', 'mom'), may hold values from -6 to 6
- coupling: bfloat16 [4, 128, 128], replicated, may hold values from -0.5 to 0.5
- pattern: int32 [12], replicated, may hold values from 0 to 3
- neighbours: int32 [4, 3], P('mom'), may hold values from -1 to 1
- offsets: int32 [32], replicated, may hold values from -8 to 8, as said below
- tap_weight: float32 [32], replicated, may hold values from 0.005 to 0.04
Outputs:
- self_energy: bfloat16 [8, 4, 2, 1536, 128], P(None, 'mom', None, 'energy')
The draws below stay inside these ranges and needn't reach their ends.
Inputs may be any that keep to these rules, and one draw needn't show every extreme that they name: `offsets`: both ends of the range are taken by some tap.
All inputs are finite; a program needn't handle non-finite values.
Results may differ from the reference program's by a relative error of at most 0.0081.
Values may be sent and summed in bfloat16 or wider, within the bound.
A program may use at most 64 MiB of HBM per device.

```python
import math
import jax
import jax.numpy as jnp
from jax import lax

ORB = 128
SLABS = 12
KINDS = 4
NBR = 3
TAPS = 32
ENERGIES = 8
MOMENTA = 4
MAXOFF = 8


def draw_offsets(key, part):
    first, second = jax.random.split(key, 2)
    values = jax.random.randint(first, (TAPS,), -MAXOFF, MAXOFF + 1)
    places = jax.random.permutation(second, TAPS)
    values = values.at[places[0]].set(MAXOFF)
    values = values.at[places[1]].set(-MAXOFF)
    return values.astype(jnp.int32)


def with_ends(values, key, low, high):
    dims = values.shape
    spot = [jax.random.randint(jax.random.fold_in(key, axis), (), 0, dims[axis]) for axis in range(len(dims))]
    values = values.at[tuple(spot)].set(low)
    longest = dims.index(max(dims))
    spot[longest] = (spot[longest] + 1) % dims[longest]
    return values.at[tuple(spot)].set(high)


def levels(key, dims, shards, low, top_value):
    def one(position, blocks):
        heights = jax.random.uniform(jax.random.fold_in(jax.random.fold_in(key, 6), position), (blocks,), jnp.float32, low / len(shards), top_value / len(shards))
        return jnp.repeat(jnp.exp(heights), dims[position] // blocks).reshape((-1,) + (1,) * (len(dims) - position - 1))

    loudness = one(*shards[0])
    for cut in shards[1:]:
        loudness = loudness * one(*cut)
    return loudness


def gaussian(rng, shape, width, most, pieces=(), kind=jnp.bfloat16):
    loudness = levels(rng, shape, pieces, -0.22, 0.18) if pieces else 1.0
    values = jax.random.normal(rng, shape, jnp.float32) * width * loudness
    return jnp.minimum(jnp.maximum(values, -most), most).astype(kind)


def setup_inputs(seed: int = 0) -> dict:
    key_of = jax.random.split(jax.random.key(seed), 8)
    return {
        "green_ret": gaussian(key_of[0], (ENERGIES, MOMENTA, SLABS, 3, 2, ORB, ORB), ORB ** -0.5, 0.5, ((0, 8), (1, 4))),
        "sigma_in": gaussian(key_of[1], (ENERGIES, MOMENTA, SLABS, 2, ORB, ORB), 1.0, 6.0, ((0, 8), (1, 4))),
        "coupling": gaussian(key_of[2], (KINDS, ORB, ORB), ORB ** -0.5, 0.5),
        "pattern": with_ends(jax.random.randint(key_of[3], (SLABS,), 0, KINDS), jax.random.fold_in(key_of[3], 1), 0, KINDS - 1).astype(jnp.int32),
        "neighbours": with_ends(jax.random.randint(key_of[4], (MOMENTA, NBR), -1, 2), jax.random.fold_in(key_of[4], 1), -1, 1).astype(jnp.int32),
        "offsets": draw_offsets(jax.random.fold_in(key_of[7], 71), 0),
        "tap_weight": jnp.clip(jnp.exp(jax.random.uniform(key_of[6], (TAPS,), jnp.float32, math.log(0.005), math.log(0.04))), 0.005, 0.04),
    }


HIGH = lax.Precision.HIGHEST


def product(left, right):
    return jnp.einsum("sab,sbc->sac", left.astype(jnp.float32), right.astype(jnp.float32), precision=HIGH)


def product_adjoint(left, right):
    return jnp.einsum("sab,scb->sac", left.astype(jnp.float32), right.astype(jnp.float32), precision=HIGH)


def slab_lesser(green, sigma, slab_coupling):
    slabs = green.shape[0]
    orbitals = green.shape[-1]
    padded = jnp.pad(sigma, ((1, 1), (0, 0), (0, 0), (0, 0)))
    total_real = jnp.zeros((slabs, orbitals, orbitals), jnp.float32)
    total_imag = jnp.zeros((slabs, orbitals, orbitals), jnp.float32)
    for term in range(3):
        near = padded[term:term + slabs]
        coupled_real = product(slab_coupling, green[:, term, 0]).astype(jnp.bfloat16)
        coupled_imag = product(slab_coupling, green[:, term, 1]).astype(jnp.bfloat16)
        left_real = (product(coupled_real, near[:, 0]) - product(coupled_imag, near[:, 1])).astype(jnp.bfloat16)
        left_imag = (product(coupled_real, near[:, 1]) + product(coupled_imag, near[:, 0])).astype(jnp.bfloat16)
        total_real = total_real + product_adjoint(left_real, coupled_real) + product_adjoint(left_imag, coupled_imag)
        total_imag = total_imag + product_adjoint(left_imag, coupled_real) - product_adjoint(left_real, coupled_imag)
    rows = slabs * orbitals
    return jnp.stack([total_real.reshape(rows, orbitals), total_imag.reshape(rows, orbitals)]).astype(jnp.bfloat16)


def reference(green_ret, sigma_in, coupling, pattern, neighbours, offsets, tap_weight):
    kinds = coupling.shape[0]
    onehot = (pattern[:, None] == jnp.arange(kinds, dtype=jnp.int32)[None, :]).astype(jnp.float32)
    slab_coupling = jnp.einsum("sk,kab->sab", onehot, coupling.astype(jnp.float32), precision=HIGH).astype(jnp.bfloat16)
    flat_green = green_ret.reshape((ENERGIES * MOMENTA,) + green_ret.shape[2:])
    flat_sigma = sigma_in.reshape((ENERGIES * MOMENTA,) + sigma_in.shape[2:])
    lesser = lax.map(lambda pair: slab_lesser(pair[0], pair[1], slab_coupling), (flat_green, flat_sigma))
    lesser = lesser.reshape((ENERGIES, MOMENTA) + lesser.shape[1:])
    counts = jnp.stack([jnp.sum((neighbours == side).astype(jnp.float32), axis=1) for side in (-1, 0, 1)], axis=1)
    index = jnp.arange(ENERGIES, dtype=jnp.int32)
    hit = index[None, :, None] == index[:, None, None] - offsets[None, None, :]
    banded = jnp.sum(jnp.where(hit, tap_weight[None, None, :], jnp.zeros((), jnp.float32)), axis=2).astype(jnp.bfloat16)

    def one_momentum(momentum):
        below = lax.dynamic_index_in_dim(lesser, ((momentum - 1) % MOMENTA).astype(jnp.int32), 1, False)
        own = lax.dynamic_index_in_dim(lesser, momentum.astype(jnp.int32), 1, False)
        above = lax.dynamic_index_in_dim(lesser, ((momentum + 1) % MOMENTA).astype(jnp.int32), 1, False)
        weights = lax.dynamic_index_in_dim(counts, momentum.astype(jnp.int32), 0, False)
        mixed = (weights[0] * below.astype(jnp.float32) + weights[1] * own.astype(jnp.float32)
                 + weights[2] * above.astype(jnp.float32)).astype(jnp.bfloat16)
        return jnp.einsum("ef,fcrk->ecrk", banded.astype(jnp.float32), mixed.astype(jnp.float32), precision=HIGH).astype(jnp.bfloat16)

    result = lax.map(one_momentum, jnp.arange(MOMENTA, dtype=jnp.int32))
    return jnp.transpose(result, (1, 0, 2, 3, 4))
```

```python
import functools
import math

import jax
import jax.numpy as jnp
from jax import lax
from jax.experimental import pallas as pl
from jax.experimental.pallas import tpu as pltpu
from jax.sharding import PartitionSpec as P

MESH = pl.DeviceIdType.MESH


def kernel(
    energies,
    momenta,
    green,
    sigma,
    coupling,
    pattern,
    neighbours,
    offsets,
    tap_weight,
    out,
    gbuf,
    sbuf,
    lesser,
    halo,
    mixed,
    gathered,
    table,
    gsem,
    ssem,
    zsend,
    zrecv,
    asend,
    arecv,
):
    slabs, _, _, orb, _ = gbuf.shape
    own_rows = gathered.shape[2]
    unit = math.gcd(orb, own_rows)
    per_slab = orb // unit
    per_owner = own_rows // unit
    me = lax.axis_index("energy")
    mom = lax.axis_index("mom")
    above = lax.rem(mom + 1, momenta)
    below = lax.rem(mom + momenta - 1, momenta)

    group = me // 2
    span = max(1, 2 * own_rows // orb)
    start = lax.rem(group * (2 * own_rows) // orb + span, slabs)

    def slab_at(step):
        return lax.rem(start + step, slabs)

    barrier = pltpu.get_barrier_semaphore()
    for to in (above, below):
        pl.semaphore_signal(barrier, inc=1, device_id={"mom": to}, device_id_type=MESH)
    for step in range(1, energies):
        to = lax.rem(me + step, energies)
        pl.semaphore_signal(barrier, inc=1, device_id={"energy": to}, device_id_type=MESH)

    sigma_copy = pltpu.make_async_copy(sigma.at[0, 0], sbuf.at[pl.ds(1, slabs)], ssem)
    sigma_copy.start()

    def green_copy(slab):
        return pltpu.make_async_copy(green.at[0, 0, slab], gbuf.at[slab], gsem.at[slab])

    @pl.loop(0, slabs)
    def _(step):
        green_copy(slab_at(step)).start()

    sbuf[0] = jnp.zeros(sbuf.shape[1:], sbuf.dtype)
    sbuf[slabs + 1] = jnp.zeros(sbuf.shape[1:], sbuf.dtype)
    sigma_copy.wait()

    def halo_copy(slab, side, to):
        return pltpu.make_async_remote_copy(
            src_ref=lesser.at[slab],
            dst_ref=halo.at[side, slab],
            send_sem=zsend.at[side, slab],
            recv_sem=zrecv.at[side, slab],
            device_id={"mom": to},
            device_id_type=MESH,
        )

    low = (mom < momenta // 2).astype(jnp.int32)
    first_to = jnp.where(low == 1, below, above)
    second_to = jnp.where(low == 1, above, below)

    @pl.loop(0, slabs)
    def _(step):
        slab = slab_at(step)
        green_copy(slab).wait()
        couple = coupling[pattern[slab]]
        total = jnp.zeros((orb, 2 * orb), jnp.float32)
        for term in range(3):
            block = jnp.concatenate([gbuf[slab, term, 0], gbuf[slab, term, 1]], axis=1)
            coupled = jnp.dot(couple, block, preferred_element_type=jnp.float32)
            coupled = coupled.astype(jnp.bfloat16)
            near_real = sbuf[slab + term, 0]
            near_imag = sbuf[slab + term, 1]
            near = jnp.concatenate(
                [
                    jnp.concatenate([near_real, near_imag], axis=1),
                    jnp.concatenate([-near_imag, near_real], axis=1),
                ],
                axis=0,
            )
            left = jnp.dot(coupled, near, preferred_element_type=jnp.float32)
            left = left.astype(jnp.bfloat16)
            turned = jnp.concatenate([-coupled[:, orb:], coupled[:, :orb]], axis=1)
            adjoint = jnp.concatenate([coupled, turned], axis=0)
            total = total + lax.dot_general(
                left, adjoint, (((1,), (1,)), ((), ())), preferred_element_type=jnp.float32
            )
        total = total.astype(jnp.bfloat16)
        lesser[slab, 0] = total[:, :orb]
        lesser[slab, 1] = total[:, orb:]

        @pl.when(step == 0)
        def _():
            pl.semaphore_wait(barrier, energies + 1)

        halo_copy(slab, low, first_to).start()
        halo_copy(slab, 1 - low, second_to).start()

    shift = lax.broadcasted_iota(jnp.int32, table.shape, 0) - (energies - 1)
    summed = jnp.zeros(table.shape, jnp.float32)
    for tap in range(offsets.shape[0]):
        summed = summed + jnp.where(shift == offsets[tap], tap_weight[tap], 0.0)
    table[...] = summed.astype(jnp.bfloat16).astype(jnp.float32)

    def count(side):
        total = jnp.float32(0.0)
        for entry in range(neighbours.shape[1]):
            total = total + jnp.where(neighbours[0, entry] == side, 1.0, 0.0)
        return total

    weights = [count(side) for side in (-1, 0, 1)]

    def mixed_copy(slab, part, to, source, place):
        return pltpu.make_async_remote_copy(
            src_ref=mixed.at[slab, :, pl.ds(part * unit, unit), :],
            dst_ref=gathered.at[source, :, pl.ds(place * unit, unit), :],
            send_sem=asend.at[slab, part],
            recv_sem=arecv.at[source, place],
            device_id={"energy": to},
            device_id_type=MESH,
        )

    @pl.loop(0, slabs)
    def _(step):
        slab = slab_at(step)
        halo_copy(slab, 0, above).wait_recv()
        halo_copy(slab, 1, below).wait_recv()
        for part in range(per_slab):
            rows = pl.ds(part * unit, unit)
            value = weights[0] * halo[0, slab, :, rows, :].astype(jnp.float32)
            value = value + weights[1] * lesser[slab, :, rows, :].astype(jnp.float32)
            value = value + weights[2] * halo[1, slab, :, rows, :].astype(jnp.float32)
            value = value.astype(jnp.bfloat16)
            piece = slab * per_slab + part
            owner = piece // per_owner
            place = lax.rem(piece, per_owner)

            @pl.when(owner == me)
            def _():
                gathered[me, :, pl.ds(pl.multiple_of(place * unit, unit), unit), :] = value

            @pl.when(owner != me)
            def _():
                mixed[slab, :, rows, :] = value
                mixed_copy(slab, part, owner, me, place).start()

    for place in range(per_owner):
        for step in range(1, energies):
            source = lax.rem(me + step, energies)
            mixed_copy(0, 0, source, source, place).wait_recv()

        block = 16
        blocks = unit // block

        @pl.loop(0, 2 * blocks)
        def _(index):
            part = index // blocks
            rows = pl.ds(
                pl.multiple_of(place * unit + lax.rem(index, blocks) * block, block), block
            )
            values = [gathered[f, part, rows, :].astype(jnp.float32) for f in range(energies)]
            for e in range(energies):
                total = None
                for f in range(energies):
                    term = table[pl.ds(e - f + energies - 1, 1), :] * values[f]
                    total = term if total is None else total + term
                out[e, 0, part, rows, :] = total.astype(jnp.bfloat16)

    @pl.loop(0, slabs)
    def _(slab):
        halo_copy(slab, 0, above).wait_send()
        halo_copy(slab, 1, below).wait_send()
        for part in range(per_slab):
            piece = slab * per_slab + part
            owner = piece // per_owner

            @pl.when(owner != me)
            def _():
                mixed_copy(slab, part, owner, me, lax.rem(piece, per_owner)).wait_send()


def shards(green_ret, sigma_in, coupling, pattern, neighbours, offsets, tap_weight):
    energies = lax.axis_size("energy")
    momenta = lax.axis_size("mom")
    slabs = green_ret.shape[2]
    orb = green_ret.shape[-1]
    own_rows = slabs * orb // energies
    unit = math.gcd(orb, own_rows)
    table_rows = -(-(2 * energies - 1) // 8) * 8
    any_space = pl.BlockSpec(memory_space=pl.ANY)
    vmem = pl.BlockSpec(memory_space=pltpu.VMEM)
    smem = pl.BlockSpec(memory_space=pltpu.SMEM)
    bf16 = jnp.bfloat16
    products = 30 * slabs * orb**3
    return pl.pallas_call(
        functools.partial(kernel, energies, momenta),
        out_shape=jax.ShapeDtypeStruct((energies, 1, 2, own_rows, orb), bf16),
        in_specs=[any_space, any_space, vmem, smem, smem, smem, smem],
        out_specs=vmem,
        scratch_shapes=[
            pltpu.VMEM((slabs, 3, 2, orb, orb), bf16),
            pltpu.VMEM((slabs + 2, 2, orb, orb), bf16),
            pltpu.VMEM((slabs, 2, orb, orb), bf16),
            pltpu.VMEM((2, slabs, 2, orb, orb), bf16),
            pltpu.VMEM((slabs, 2, orb, orb), bf16),
            pltpu.VMEM((energies, 2, own_rows, orb), bf16),
            pltpu.VMEM((table_rows, orb), jnp.float32),
            pltpu.SemaphoreType.DMA((slabs,)),
            pltpu.SemaphoreType.DMA,
            pltpu.SemaphoreType.DMA((2, slabs)),
            pltpu.SemaphoreType.DMA((2, slabs)),
            pltpu.SemaphoreType.DMA((slabs, orb // unit)),
            pltpu.SemaphoreType.DMA((energies, own_rows // unit)),
        ],
        compiler_params=pltpu.CompilerParams(
            collective_id=0, has_side_effects=True, vmem_limit_bytes=32 * 1024 * 1024
        ),
        cost_estimate=pl.CostEstimate(
            flops=2 * products, bytes_accessed=8 * slabs * orb * orb * 2, transcendentals=0
        ),
    )(green_ret, sigma_in, coupling, pattern, neighbours, offsets, tap_weight)


def solution(mesh):
    return jax.shard_map(
        shards,
        mesh=mesh,
        in_specs=(
            P("energy", "mom", None, None, None, None, None),
            P("energy", "mom", None, None, None, None),
            P(),
            P(),
            P("mom", None),
            P(),
            P(),
        ),
        out_specs=P(None, "mom", None, "energy", None),
        check_vma=False,
    )
```

```python
import functools
import math

import jax
import jax.numpy as jnp
from jax import lax
from jax.experimental import pallas as pl
from jax.experimental.pallas import tpu as pltpu
from jax.sharding import PartitionSpec as P

MESH = pl.DeviceIdType.MESH


def kernel(
    energies,
    momenta,
    green,
    sigma,
    coupling_in,
    pattern_in,
    neighbours_in,
    offsets_in,
    tap_weight_in,
    out,
    coupling,
    pattern,
    neighbours,
    offsets,
    tap_weight,
    gbuf,
    sbuf,
    lesser,
    halo,
    mixed,
    gathered,
    table,
    small_sem,
    gsem,
    ssem,
    zsend,
    zrecv,
    asend,
    arecv,
):
    slabs, _, _, orb, _ = gbuf.shape
    own_rows = gathered.shape[2]
    unit = math.gcd(orb, own_rows)
    per_slab = orb // unit
    per_owner = own_rows // unit
    me = lax.axis_index("energy")
    mom = lax.axis_index("mom")
    above = lax.rem(mom + 1, momenta)
    below = lax.rem(mom + momenta - 1, momenta)

    span = max(1, 2 * own_rows // orb)
    span = span if slabs % span == 0 else 1
    inner = sorted(range(span), key=lambda place: -abs(2 * place - span + 1))

    def start_of(device):
        return ((device // 2) * (2 * own_rows) // orb + span) % slabs

    start = lax.rem((me // 2) * (2 * own_rows) // orb + span, slabs)

    def slab_at(step):
        inside = lax.rem(step, span)
        moved = sum(jnp.where(inside == i, inner[i], 0) for i in range(span))
        return lax.rem(start + step - inside + moved, slabs)

    def place_of(device, turn):
        return turn if device % 2 == 0 else per_owner - 1 - turn

    step_of = [i - i % span + inner.index(i % span) for i in range(slabs)]
    last_step = []
    for turn in range(per_owner):
        latest = 0
        for owner in range(energies):
            piece = owner * per_owner + place_of(owner, turn)
            for source in range(energies):
                latest = max(latest, step_of[(piece // per_slab - start_of(source)) % slabs])
        last_step.append(latest)

    barrier = pltpu.get_barrier_semaphore()
    for to in (above, below):
        pl.semaphore_signal(barrier, inc=1, device_id={"mom": to}, device_id_type=MESH)
    for step in range(1, energies):
        to = lax.rem(me + step, energies)
        pl.semaphore_signal(barrier, inc=1, device_id={"energy": to}, device_id_type=MESH)

    sigma_copy = pltpu.make_async_copy(sigma.at[0, 0], sbuf.at[pl.ds(1, slabs)], ssem)
    sigma_copy.start()

    def green_copy(slab):
        return pltpu.make_async_copy(green.at[0, 0, slab], gbuf.at[slab], gsem.at[slab])

    @pl.loop(0, slabs)
    def _(step):
        green_copy(slab_at(step)).start()

    small = [
        pltpu.make_async_copy(source, target, small_sem.at[i])
        for i, (source, target) in enumerate(
            [
                (coupling_in, coupling),
                (pattern_in, pattern),
                (neighbours_in, neighbours),
                (offsets_in, offsets),
                (tap_weight_in, tap_weight),
            ]
        )
    ]
    for copy in small:
        copy.start()

    sbuf[0] = jnp.zeros(sbuf.shape[1:], sbuf.dtype)
    sbuf[slabs + 1] = jnp.zeros(sbuf.shape[1:], sbuf.dtype)
    for copy in small:
        copy.wait()
    sigma_copy.wait()

    def halo_copy(slab, side, to):
        return pltpu.make_async_remote_copy(
            src_ref=lesser.at[slab],
            dst_ref=halo.at[side, slab],
            send_sem=zsend.at[side, slab],
            recv_sem=zrecv.at[side, slab],
            device_id={"mom": to},
            device_id_type=MESH,
        )

    low = (mom < momenta // 2).astype(jnp.int32)
    first_to = jnp.where(low == 1, below, above)
    second_to = jnp.where(low == 1, above, below)

    @pl.loop(0, slabs)
    def _(step):
        slab = slab_at(step)
        green_copy(slab).wait()
        couple = coupling[pattern[slab]]
        total = jnp.zeros((orb, 2 * orb), jnp.float32)
        for term in range(3):
            block = jnp.concatenate([gbuf[slab, term, 0], gbuf[slab, term, 1]], axis=1)
            coupled = jnp.dot(couple, block, preferred_element_type=jnp.float32)
            coupled = coupled.astype(jnp.bfloat16)
            near_real = sbuf[slab + term, 0]
            near_imag = sbuf[slab + term, 1]
            near = jnp.concatenate(
                [
                    jnp.concatenate([near_real, near_imag], axis=1),
                    jnp.concatenate([-near_imag, near_real], axis=1),
                ],
                axis=0,
            )
            left = jnp.dot(coupled, near, preferred_element_type=jnp.float32)
            left = left.astype(jnp.bfloat16)
            turned = jnp.concatenate([-coupled[:, orb:], coupled[:, :orb]], axis=1)
            adjoint = jnp.concatenate([coupled, turned], axis=0)
            total = total + lax.dot_general(
                left, adjoint, (((1,), (1,)), ((), ())), preferred_element_type=jnp.float32
            )
        total = total.astype(jnp.bfloat16)
        lesser[slab, 0] = total[:, :orb]
        lesser[slab, 1] = total[:, orb:]

        @pl.when(step == 0)
        def _():
            pl.semaphore_wait(barrier, energies + 1)

        halo_copy(slab, low, first_to).start()
        halo_copy(slab, 1 - low, second_to).start()

    shift = lax.broadcasted_iota(jnp.int32, table.shape, 0) - (energies - 1)
    summed = jnp.zeros(table.shape, jnp.float32)
    for tap in range(offsets.shape[0]):
        summed = summed + jnp.where(shift == offsets[tap], tap_weight[tap], 0.0)
    table[...] = summed.astype(jnp.bfloat16).astype(jnp.float32)

    def count(side):
        total = jnp.float32(0.0)
        for entry in range(neighbours.shape[1]):
            total = total + jnp.where(neighbours[0, entry] == side, 1.0, 0.0)
        return total

    weights = [count(side) for side in (-1, 0, 1)]

    def mixed_copy(slab, part, to, source, place):
        return pltpu.make_async_remote_copy(
            src_ref=mixed.at[slab, :, pl.ds(part * unit, unit), :],
            dst_ref=gathered.at[source, :, pl.ds(place * unit, unit), :],
            send_sem=asend.at[slab, part],
            recv_sem=arecv.at[source, place],
            device_id={"energy": to},
            device_id_type=MESH,
        )

    def mix(step):
        slab = slab_at(step)
        halo_copy(slab, 0, above).wait_recv()
        halo_copy(slab, 1, below).wait_recv()
        for part in range(per_slab):
            rows = pl.ds(part * unit, unit)
            value = weights[0] * halo[0, slab, :, rows, :].astype(jnp.float32)
            value = value + weights[1] * lesser[slab, :, rows, :].astype(jnp.float32)
            value = value + weights[2] * halo[1, slab, :, rows, :].astype(jnp.float32)
            value = value.astype(jnp.bfloat16)
            piece = slab * per_slab + part
            owner = piece // per_owner
            place = lax.rem(piece, per_owner)

            @pl.when(owner == me)
            def _():
                gathered[me, :, pl.ds(pl.multiple_of(place * unit, unit), unit), :] = value

            @pl.when(owner != me)
            def _():
                mixed[slab, :, rows, :] = value
                mixed_copy(slab, part, owner, me, place).start()

    block = 16
    blocks = unit // block

    def band(turn):
        place = jnp.where(lax.rem(me, 2) == 0, turn, per_owner - 1 - turn)
        for step in range(1, energies):
            source = lax.rem(me + step, energies)
            mixed_copy(0, 0, source, source, place).wait_recv()

        @pl.loop(0, 2 * blocks)
        def _(index):
            part = index // blocks
            rows = pl.ds(
                pl.multiple_of(place * unit + lax.rem(index, blocks) * block, block), block
            )
            values = [gathered[f, part, rows, :].astype(jnp.float32) for f in range(energies)]
            for e in range(energies):
                total = None
                for f in range(energies):
                    term = table[pl.ds(e - f + energies - 1, 1), :] * values[f]
                    total = term if total is None else total + term
                out[e, 0, part, rows, :] = total.astype(jnp.bfloat16)

    done = 0
    for turn in range(per_owner):
        upto = max(done, last_step[turn] + 1)
        if upto > done:
            pl.loop(done, upto)(mix)
        done = upto
        band(turn)
    if done < slabs:
        pl.loop(done, slabs)(mix)

    @pl.loop(0, slabs)
    def _(slab):
        halo_copy(slab, 0, above).wait_send()
        halo_copy(slab, 1, below).wait_send()
        for part in range(per_slab):
            piece = slab * per_slab + part
            owner = piece // per_owner

            @pl.when(owner != me)
            def _():
                mixed_copy(slab, part, owner, me, lax.rem(piece, per_owner)).wait_send()


def shards(green_ret, sigma_in, coupling, pattern, neighbours, offsets, tap_weight):
    energies = lax.axis_size("energy")
    momenta = lax.axis_size("mom")
    slabs = green_ret.shape[2]
    orb = green_ret.shape[-1]
    own_rows = slabs * orb // energies
    unit = math.gcd(orb, own_rows)
    table_rows = -(-(2 * energies - 1) // 8) * 8
    hbm = pl.BlockSpec(memory_space=pltpu.HBM)
    vmem = pl.BlockSpec(memory_space=pltpu.VMEM)
    bf16 = jnp.bfloat16
    products = 30 * slabs * orb**3
    return pl.pallas_call(
        functools.partial(kernel, energies, momenta),
        out_shape=pltpu.VMEM((energies, 1, 2, own_rows, orb), bf16),
        in_specs=[hbm] * 7,
        out_specs=vmem,
        scratch_shapes=[
            pltpu.VMEM(coupling.shape, bf16),
            pltpu.SMEM(pattern.shape, jnp.int32),
            pltpu.SMEM(neighbours.shape, jnp.int32),
            pltpu.SMEM(offsets.shape, jnp.int32),
            pltpu.SMEM(tap_weight.shape, jnp.float32),
            pltpu.VMEM((slabs, 3, 2, orb, orb), bf16),
            pltpu.VMEM((slabs + 2, 2, orb, orb), bf16),
            pltpu.VMEM((slabs, 2, orb, orb), bf16),
            pltpu.VMEM((2, slabs, 2, orb, orb), bf16),
            pltpu.VMEM((slabs, 2, orb, orb), bf16),
            pltpu.VMEM((energies, 2, own_rows, orb), bf16),
            pltpu.VMEM((table_rows, orb), jnp.float32),
            pltpu.SemaphoreType.DMA((5,)),
            pltpu.SemaphoreType.DMA((slabs,)),
            pltpu.SemaphoreType.DMA,
            pltpu.SemaphoreType.DMA((2, slabs)),
            pltpu.SemaphoreType.DMA((2, slabs)),
            pltpu.SemaphoreType.DMA((slabs, orb // unit)),
            pltpu.SemaphoreType.DMA((energies, own_rows // unit)),
        ],
        compiler_params=pltpu.CompilerParams(
            collective_id=0, has_side_effects=True, vmem_limit_bytes=40 * 1024 * 1024
        ),
        cost_estimate=pl.CostEstimate(
            flops=2 * products, bytes_accessed=8 * slabs * orb * orb * 2, transcendentals=0
        ),
    )(*[pltpu.with_memory_space_constraint(x, pltpu.HBM) for x in (green_ret, sigma_in, coupling, pattern, neighbours, offsets, tap_weight)])


def solution(mesh):
    return jax.shard_map(
        shards,
        mesh=mesh,
        in_specs=(
            P("energy", "mom", None, None, None, None, None),
            P("energy", "mom", None, None, None, None),
            P(),
            P(),
            P("mom", None),
            P(),
            P(),
        ),
        out_specs=P(None, "mom", None, "energy", None),
        check_vma=False,
    )
```

```python
import functools
import math

import jax
import jax.numpy as jnp
from jax import lax
from jax.experimental import pallas as pl
from jax.experimental.pallas import tpu as pltpu
from jax.sharding import PartitionSpec as P

MESH = pl.DeviceIdType.MESH


def kernel(
    energies,
    momenta,
    green,
    sigma,
    coupling_in,
    pattern_in,
    neighbours_in,
    offsets_in,
    tap_weight_in,
    out,
    coupling,
    pattern,
    neighbours,
    offsets,
    tap_weight,
    gbuf,
    sbuf,
    lesser,
    halo,
    relay,
    mixed,
    gathered,
    table,
    small_sem,
    gsem,
    ssem,
    zsend,
    zrecv,
    rsend,
    rrecv,
    asend,
    arecv,
):
    slabs, _, _, orb, _ = gbuf.shape
    own_rows = gathered.shape[2]
    unit = math.gcd(orb, own_rows)
    per_slab = orb // unit
    per_owner = own_rows // unit
    me = lax.axis_index("energy")
    mom = lax.axis_index("mom")
    above = lax.rem(mom + 1, momenta)
    below = lax.rem(mom + momenta - 1, momenta)

    span = max(1, 2 * own_rows // orb)
    span = span if slabs % span == 0 else 1
    inner = sorted(range(span), key=lambda place: -abs(2 * place - span + 1))

    start = lax.rem((me // 2) * (2 * own_rows) // orb + span, slabs)

    def slab_at(step):
        inside = lax.rem(step, span)
        moved = sum(jnp.where(inside == i, inner[i], 0) for i in range(span))
        return lax.rem(start + step - inside + moved, slabs)

    small = [
        pltpu.make_async_copy(source, target, small_sem.at[i])
        for i, (source, target) in enumerate(
            [
                (coupling_in, coupling),
                (pattern_in, pattern),
                (neighbours_in, neighbours),
                (offsets_in, offsets),
                (tap_weight_in, tap_weight),
            ]
        )
    ]
    for copy in small:
        copy.start()

    barrier = pltpu.get_barrier_semaphore()
    for to in (above, below):
        pl.semaphore_signal(barrier, inc=1, device_id={"mom": to}, device_id_type=MESH)
    for step in range(1, energies):
        to = lax.rem(me + step, energies)
        pl.semaphore_signal(barrier, inc=1, device_id={"energy": to}, device_id_type=MESH)

    sigma_copy = pltpu.make_async_copy(sigma.at[0, 0], sbuf.at[pl.ds(1, slabs)], ssem)
    sigma_copy.start()

    def green_copy(slab):
        return pltpu.make_async_copy(green.at[0, 0, slab], gbuf.at[slab], gsem.at[slab])

    @pl.loop(0, slabs)
    def _(step):
        green_copy(slab_at(step)).start()

    sbuf[0] = jnp.zeros(sbuf.shape[1:], sbuf.dtype)
    sbuf[slabs + 1] = jnp.zeros(sbuf.shape[1:], sbuf.dtype)
    for copy in small:
        copy.wait()
    sigma_copy.wait()

    def halo_copy(slab, side, to):
        return pltpu.make_async_remote_copy(
            src_ref=lesser.at[slab],
            dst_ref=halo.at[side, slab],
            send_sem=zsend.at[side, slab],
            recv_sem=zrecv.at[side, slab],
            device_id={"mom": to},
            device_id_type=MESH,
        )

    low = (mom < momenta // 2).astype(jnp.int32)
    outward = jnp.where(low == 1, below, above)
    inward = jnp.where(low == 1, above, below)

    line = momenta == 4
    inside = (mom == 1) | (mom == 2)

    def to_inward(step):
        return halo_copy(slab_at(step), 1 - low, inward)

    def to_outward(step):
        return halo_copy(slab_at(step), low, outward)

    def relay_in(step):
        slab = slab_at(step)
        return pltpu.make_async_remote_copy(
            src_ref=halo.at[1 - low, slab],
            dst_ref=relay.at[slab],
            send_sem=rsend.at[0, slab],
            recv_sem=rrecv.at[slab],
            device_id={"mom": inward},
            device_id_type=MESH,
        )

    def relay_out(step):
        slab = slab_at(step)
        return pltpu.make_async_remote_copy(
            src_ref=relay.at[slab],
            dst_ref=halo.at[1 - low, slab],
            send_sem=rsend.at[1, slab],
            recv_sem=zrecv.at[1 - low, slab],
            device_id={"mom": outward},
            device_id_type=MESH,
        )

    def compute(step):
        slab = slab_at(step)
        green_copy(slab).wait()
        couple = coupling[pattern[slab]]
        total = jnp.zeros((orb, 2 * orb), jnp.float32)
        for term in range(3):
            block = jnp.concatenate([gbuf[slab, term, 0], gbuf[slab, term, 1]], axis=1)
            coupled = jnp.dot(couple, block, preferred_element_type=jnp.float32)
            coupled = coupled.astype(jnp.bfloat16)
            near_real = sbuf[slab + term, 0]
            near_imag = sbuf[slab + term, 1]
            near = jnp.concatenate(
                [
                    jnp.concatenate([near_real, near_imag], axis=1),
                    jnp.concatenate([-near_imag, near_real], axis=1),
                ],
                axis=0,
            )
            left = jnp.dot(coupled, near, preferred_element_type=jnp.float32)
            left = left.astype(jnp.bfloat16)
            turned = jnp.concatenate([-coupled[:, orb:], coupled[:, :orb]], axis=1)
            adjoint = jnp.concatenate([coupled, turned], axis=0)
            total = total + lax.dot_general(
                left, adjoint, (((1,), (1,)), ((), ())), preferred_element_type=jnp.float32
            )
        total = total.astype(jnp.bfloat16)
        lesser[slab, 0] = total[:, :orb]
        lesser[slab, 1] = total[:, orb:]

        @pl.when(step == 0)
        def _():
            pl.semaphore_wait(barrier, energies + 1)

    shift = lax.broadcasted_iota(jnp.int32, table.shape, 0) - (energies - 1)
    summed = jnp.zeros(table.shape, jnp.float32)
    for tap in range(offsets.shape[0]):
        summed = summed + jnp.where(shift == offsets[tap], tap_weight[tap], 0.0)
    table[...] = summed.astype(jnp.bfloat16).astype(jnp.float32)

    def count(side):
        total = jnp.float32(0.0)
        for entry in range(neighbours.shape[1]):
            total = total + jnp.where(neighbours[0, entry] == side, 1.0, 0.0)
        return total

    weights = [count(side) for side in (-1, 0, 1)]

    def mixed_copy(slab, part, to, source, place):
        return pltpu.make_async_remote_copy(
            src_ref=mixed.at[slab, :, pl.ds(part * unit, unit), :],
            dst_ref=gathered.at[source, :, pl.ds(place * unit, unit), :],
            send_sem=asend.at[slab, part],
            recv_sem=arecv.at[source, place],
            device_id={"energy": to},
            device_id_type=MESH,
        )

    def mix(step):
        slab = slab_at(step)
        if line:
            halo_copy(slab, low, outward).wait_recv()

            @pl.when(jnp.logical_not(inside))
            def _():
                halo_copy(slab, 1 - low, inward).wait_recv()
        else:
            halo_copy(slab, 0, above).wait_recv()
            halo_copy(slab, 1, below).wait_recv()
        for part in range(per_slab):
            rows = pl.ds(part * unit, unit)
            value = weights[0] * halo[0, slab, :, rows, :].astype(jnp.float32)
            value = value + weights[1] * lesser[slab, :, rows, :].astype(jnp.float32)
            value = value + weights[2] * halo[1, slab, :, rows, :].astype(jnp.float32)
            value = value.astype(jnp.bfloat16)
            piece = slab * per_slab + part
            owner = piece // per_owner
            place = lax.rem(piece, per_owner)

            @pl.when(owner == me)
            def _():
                gathered[me, :, pl.ds(pl.multiple_of(place * unit, unit), unit), :] = value

            @pl.when(owner != me)
            def _():
                mixed[slab, :, rows, :] = value
                mixed_copy(slab, part, owner, me, place).start()

    block = 16
    blocks = unit // block

    def band(turn):
        place = jnp.where(lax.rem(me, 2) == 0, turn, per_owner - 1 - turn)
        for step in range(1, energies):
            source = lax.rem(me + step, energies)
            mixed_copy(0, 0, source, source, place).wait_recv()

        @pl.loop(0, 2 * blocks)
        def _(index):
            part = index // blocks
            rows = pl.ds(
                pl.multiple_of(place * unit + lax.rem(index, blocks) * block, block), block
            )
            values = [gathered[f, part, rows, :].astype(jnp.float32) for f in range(energies)]
            for e in range(energies):
                total = None
                for f in range(energies):
                    term = table[pl.ds(e - f + energies - 1, 1), :] * values[f]
                    total = term if total is None else total + term
                out[e, 0, part, rows, :] = total.astype(jnp.bfloat16)

    if line:
        ahead = min(2, slabs)
        lag = ahead + 3

        @pl.loop(0, slabs + lag)
        def _(tick):
            @pl.when(tick < slabs)
            def _():
                compute(tick)

                @pl.when(inside)
                def _():
                    to_outward(tick).start()

                @pl.when(jnp.logical_not(inside) | (tick < ahead))
                def _():
                    to_inward(tick).start()

            @pl.when(inside & (tick >= ahead) & (tick < slabs + ahead))
            def _():
                step = tick - ahead
                to_inward(step).wait_recv()
                relay_in(step).start()

                @pl.when(lax.rem(step, 2) == 1)
                def _():
                    to_inward(ahead + step // 2).start()

                @pl.when(step == slabs - 1)
                def _():
                    @pl.loop(ahead + slabs // 2, slabs)
                    def _(rest):
                        to_inward(rest).start()

            @pl.when(inside & (tick >= lag))
            def _():
                relay_in(tick - lag).wait_recv()
                relay_out(tick - lag).start()

            @pl.when((tick > lag) & (lax.rem(tick - lag, 2) == 1))
            def _():
                mix((tick - lag) // 2)

    else:

        @pl.loop(0, slabs)
        def _(step):
            compute(step)
            to_outward(step).start()
            to_inward(step).start()

    done = slabs // 2 if line else 0
    pl.loop(done, slabs)(mix)
    for turn in range(per_owner):
        band(turn)

    @pl.loop(0, slabs)
    def _(slab):
        halo_copy(slab, 1 - low, inward).wait_send()
        if line:

            @pl.when(inside)
            def _():
                halo_copy(slab, low, outward).wait_send()
                relay_in(slab).wait_send()
                relay_out(slab).wait_send()
        else:
            halo_copy(slab, low, outward).wait_send()
        for part in range(per_slab):
            piece = slab * per_slab + part
            owner = piece // per_owner

            @pl.when(owner != me)
            def _():
                mixed_copy(slab, part, owner, me, lax.rem(piece, per_owner)).wait_send()


def shards(green_ret, sigma_in, coupling, pattern, neighbours, offsets, tap_weight):
    energies = lax.axis_size("energy")
    momenta = lax.axis_size("mom")
    slabs = green_ret.shape[2]
    orb = green_ret.shape[-1]
    own_rows = slabs * orb // energies
    unit = math.gcd(orb, own_rows)
    table_rows = -(-(2 * energies - 1) // 8) * 8
    hbm = pl.BlockSpec(memory_space=pltpu.HBM)
    vmem = pl.BlockSpec(memory_space=pltpu.VMEM)
    bf16 = jnp.bfloat16
    products = 30 * slabs * orb**3
    return pl.pallas_call(
        functools.partial(kernel, energies, momenta),
        out_shape=pltpu.VMEM((energies, 1, 2, own_rows, orb), bf16),
        in_specs=[hbm] * 7,
        out_specs=vmem,
        scratch_shapes=[
            pltpu.VMEM(coupling.shape, bf16),
            pltpu.SMEM(pattern.shape, jnp.int32),
            pltpu.SMEM(neighbours.shape, jnp.int32),
            pltpu.SMEM(offsets.shape, jnp.int32),
            pltpu.SMEM(tap_weight.shape, jnp.float32),
            pltpu.VMEM((slabs, 3, 2, orb, orb), bf16),
            pltpu.VMEM((slabs + 2, 2, orb, orb), bf16),
            pltpu.VMEM((slabs, 2, orb, orb), bf16),
            pltpu.VMEM((2, slabs, 2, orb, orb), bf16),
            pltpu.VMEM((slabs, 2, orb, orb), bf16),
            pltpu.VMEM((slabs, 2, orb, orb), bf16),
            pltpu.VMEM((energies, 2, own_rows, orb), bf16),
            pltpu.VMEM((table_rows, orb), jnp.float32),
            pltpu.SemaphoreType.DMA((5,)),
            pltpu.SemaphoreType.DMA((slabs,)),
            pltpu.SemaphoreType.DMA,
            pltpu.SemaphoreType.DMA((2, slabs)),
            pltpu.SemaphoreType.DMA((2, slabs)),
            pltpu.SemaphoreType.DMA((2, slabs)),
            pltpu.SemaphoreType.DMA((slabs,)),
            pltpu.SemaphoreType.DMA((slabs, orb // unit)),
            pltpu.SemaphoreType.DMA((energies, own_rows // unit)),
        ],
        compiler_params=pltpu.CompilerParams(
            collective_id=0, has_side_effects=True, vmem_limit_bytes=40 * 1024 * 1024
        ),
        cost_estimate=pl.CostEstimate(
            flops=2 * products, bytes_accessed=8 * slabs * orb * orb * 2, transcendentals=0
        ),
    )(*[pltpu.with_memory_space_constraint(x, pltpu.HBM) for x in (green_ret, sigma_in, coupling, pattern, neighbours, offsets, tap_weight)])


def solution(mesh):
    return jax.shard_map(
        shards,
        mesh=mesh,
        in_specs=(
            P("energy", "mom", None, None, None, None, None),
            P("energy", "mom", None, None, None, None),
            P(),
            P(),
            P("mom", None),
            P(),
            P(),
        ),
        out_specs=P(None, "mom", None, "energy", None),
        check_vma=False,
    )
```
